256 devices in a mesh: dp: 32 (over z, x), mp: 8 (over y, core).
Axes of the slice: x: 4, y: 4, z: 8, core: 2. Of those that a mesh axis runs over, the one named last changes fastest.
Arguments:
- queries: bfloat16 [4096, 8192], P('dp', 'mp'), may hold values from -8 to 8
- grad_out: bfloat16 [4096, 8192], P('dp', 'mp'), may hold values from -6 to 6
- row_dest: int32 [4096], P('dp'), may hold values from 0 to 31, as said below
- row_slot: int32 [4096], P('dp'), may hold values from 0 to 127, as said below
- block_image: int32 [128], P('dp'), may hold values from 0 to 31, as said below
- image_owner: int32 [32], replicated, may hold values from 0 to 31, as said below
- image_tiles: int32 [32], P('dp'), may hold values from 1 to 4, as said below
- img_keys: bfloat16 [32, 6656, 1024], P('dp', None, 'mp'), may hold values from -8 to 8
- img_values: bfloat16 [32, 6656, 1024], P('dp', None, 'mp'), may hold values from -6 to 6
Outputs:
- attended: bfloat16 [4096, 8192], P('dp', 'mp')
- grad_queries: bfloat16 [4096, 8192], P('dp', 'mp')
- grad_keys: bfloat16 [32, 6656, 1024], P('dp', None, 'mp')
- grad_values: bfloat16 [32, 6656, 1024], P('dp', None, 'mp')
The draws below stay inside these ranges and needn't reach their ends.
Inputs may be any that keep to these rules, and one draw needn't show every extreme that they name: `row_dest`: one index of dp sends at most 8 rows to any one index, exactly 8 to some; every index receives exactly 128 rows; the row counts that an index sends to the others are the same numbers on every index, assigned to other destinations. `row_slot`: the rows assigned to one index take distinct positions. `block_image`: block b lies on index b // 4 of dp and cites an image held by that index or by the next one (index + 1, modulo the axis); on every index one or two blocks cite the next one; every image is cited by at most 5 blocks, and some image by exactly so many. `image_owner`: A permutation of the indices of dp. `image_tiles`: some image has 4 tiles.
All inputs are finite; a program needn't handle non-finite values.
Results may differ from the reference program's by a relative error of at most 0.015.
Values may be sent and summed in bfloat16 or wider, within the bound.
A program may use at most 128 MiB of HBM per device.

```python
import jax
import jax.numpy as jnp
from jax import lax

HQ = 64
KVH = 8
HD = 128
TILES = 4
TILE_TOK = 1601
TOKP = 1664
TB = 32
TOK_DEV = 128
TOKENS = 4096
IMAGES = 32
BLOCKS = 128
KEYS = 6656
GROUP = 8
CAP = 8


def route_tables(key):
    ranks = IMAGES
    half_cap = CAP // 2
    subkeys = jax.random.split(jax.random.fold_in(key, 202), 5)
    placing = jax.random.permutation(subkeys[0], ranks).astype(jnp.int32)
    inverse = jnp.argsort(placing).astype(jnp.int32)
    offsets = jax.random.permutation(subkeys[1], ranks).astype(jnp.int32)
    swing = jax.random.randint(subkeys[2], ((ranks - 2) // 2,), -half_cap, half_cap + 1)
    paired = jnp.stack([half_cap + swing, half_cap - swing], axis=1).reshape(-1).astype(jnp.int32)
    amounts = jnp.concatenate([jnp.array([CAP, 0], jnp.int32), paired])
    ends = jnp.cumsum(amounts)
    which = jnp.searchsorted(ends, jnp.arange(TOK_DEV), side='right').astype(jnp.int32)
    targets = placing[(inverse[:, None] + offsets[which][None, :]) % ranks]
    shuffles = jax.vmap(lambda subkey: jax.random.permutation(subkey, TOK_DEV))(jax.random.split(subkeys[3], ranks))
    targets = jnp.take_along_axis(targets, shuffles, axis=1).reshape(-1).astype(jnp.int32)
    noise = jax.random.permutation(subkeys[4], TOKENS).astype(jnp.int32)
    ordering = jnp.argsort(targets * TOKENS + noise)
    ranking = jnp.argsort(ordering).astype(jnp.int32)
    slots = (ranking - targets * TOK_DEV).astype(jnp.int32)
    return (targets, slots)


def image_tables(key):
    ranks = IMAGES
    per_rank = BLOCKS // IMAGES
    subkeys = jax.random.split(jax.random.fold_in(key, 101), 3)
    owners = jax.random.permutation(subkeys[0], ranks).astype(jnp.int32)
    holder = jnp.argsort(owners).astype(jnp.int32)
    flips = jax.random.randint(subkeys[1], (ranks,), 0, 2).at[0].set(1).at[1].set(0)
    far_count = 1 + flips
    spots = jax.vmap(lambda subkey: jax.random.permutation(subkey, per_rank))(jax.random.split(subkeys[2], ranks))
    step_up = (spots < far_count[:, None]).astype(jnp.int32)
    target = (jnp.arange(ranks)[:, None] + step_up) % ranks
    return (holder[target].reshape(-1).astype(jnp.int32), owners)


def draw_row_dest(key, part):
    tables = route_tables(key)
    return tables[0]


def draw_row_slot(key, part):
    tables = route_tables(key)
    return tables[1]


def draw_block_image(key, part):
    tables = image_tables(key)
    return tables[0]


def draw_image_owner(key, part):
    tables = image_tables(key)
    return tables[1]


def draw_image_tiles(key, part):
    key = jax.random.fold_in(key, 3)
    first_key, second_key = jax.random.split(key)
    counts = jax.random.randint(first_key, (IMAGES,), 1, TILES + 1)
    chosen = jax.random.randint(second_key, (), 0, IMAGES)
    return counts.at[chosen].set(TILES).astype(jnp.int32)


def draw_queries(key, part):
    key = jax.random.fold_in(key, 5)
    base = jnp.clip(jax.random.normal(key, (TOKENS, HQ * HD), jnp.float32), -6.0, 6.0)
    return base.astype(jnp.bfloat16)


def draw_img_keys(key, part):
    key = jax.random.fold_in(key, 7)
    first_key = jax.random.fold_in(key, 0)
    base = jnp.clip(jax.random.normal(first_key, (IMAGES, KEYS, KVH * HD), jnp.float32), -6.0, 6.0)
    return base.astype(jnp.bfloat16)


def level_of(rng, extent, cuts, low, largest):
    level, own = 1.0, jax.random.fold_in(rng, 6)
    for dim, parts in cuts:
        steps = jnp.exp(jax.random.uniform(jax.random.fold_in(own, dim), (parts,), jnp.float32, low / len(cuts), largest / len(cuts)))
        level = level * jnp.repeat(steps, extent[dim] // parts).reshape([-1 if axis == dim else 1 for axis in range(len(extent))])
    return level


def normal_values(key, extent, width, bound, pieces=(), dtype=jnp.bfloat16):
    factor_of = level_of(key, extent, pieces, -0.22, 0.18) if pieces else 1.0
    values = jax.random.normal(key, extent, jnp.float32) * width * factor_of
    return jnp.minimum(jnp.maximum(values, -bound), bound).astype(dtype)


def setup_inputs(seed: int = 0) -> dict:
    key_list = jax.random.split(jax.random.key(seed), 10)
    queries = draw_queries(jax.random.fold_in(key_list[9], 71), 0)
    grad_out = normal_values(key_list[1], (TOKENS, HQ * HD), 1.0, 6.0, ((0, 32), (1, 8)))
    row_dest = draw_row_dest(jax.random.fold_in(key_list[9], 71), 0)
    row_slot = draw_row_slot(jax.random.fold_in(key_list[9], 71), 0)
    block_image = draw_block_image(jax.random.fold_in(key_list[9], 71), 0)
    image_owner = draw_image_owner(jax.random.fold_in(key_list[9], 71), 0)
    image_tiles = draw_image_tiles(jax.random.fold_in(key_list[9], 71), 0)
    img_keys = draw_img_keys(jax.random.fold_in(key_list[9], 71), 0)
    img_values = normal_values(key_list[8], (IMAGES, KEYS, KVH * HD), 1.0, 6.0, ((0, 32), (2, 8)))
    return {"queries": queries, "grad_out": grad_out, "row_dest": row_dest, "row_slot": row_slot, "block_image": block_image, "image_owner": image_owner, "image_tiles": image_tiles, "img_keys": img_keys, "img_values": img_values}


def head_pass(query_rows, grad_rows, key_rows, value_rows, valid_keys):
    score_scale = HD ** -0.5
    scores = lax.dot_general(query_rows, key_rows, (((1,), (1,)), ((), ())), preferred_element_type=jnp.float32) * score_scale
    masked = jnp.where(valid_keys[None, :], scores, -jnp.inf)
    top_score = jnp.max(masked, axis=1, keepdims=True)
    weights = jnp.where(valid_keys[None, :], jnp.exp(scores - top_score), 0.0)
    probs = weights / jnp.sum(weights, axis=1, keepdims=True)
    probs_low = probs.astype(jnp.bfloat16)
    attended = jnp.dot(probs_low, value_rows, preferred_element_type=jnp.float32)
    grad_value = lax.dot_general(probs_low, grad_rows, (((0,), (0,)), ((), ())), preferred_element_type=jnp.float32)
    grad_probs = lax.dot_general(grad_rows, value_rows, (((1,), (1,)), ((), ())), preferred_element_type=jnp.float32)
    row_delta = jnp.sum(grad_rows.astype(jnp.float32) * attended, axis=1, keepdims=True)
    grad_scores = (probs * (grad_probs - row_delta) * score_scale).astype(jnp.bfloat16)
    grad_query = jnp.dot(grad_scores, key_rows, preferred_element_type=jnp.float32)
    grad_key = lax.dot_general(grad_scores, query_rows, (((0,), (0,)), ((), ())), preferred_element_type=jnp.float32)
    return attended, grad_query, grad_key, grad_value


def reference(queries, grad_out, row_dest, row_slot, block_image, image_owner, image_tiles, img_keys, img_values):
    place = (row_dest * TOK_DEV + row_slot).astype(jnp.int32)
    query_bal = jnp.zeros_like(queries).at[place].set(queries)
    grad_bal = jnp.zeros_like(grad_out).at[place].set(grad_out)
    owners = image_owner[block_image].astype(jnp.int32)
    tile_counts = image_tiles[owners].astype(jnp.int32)
    query_blocks = query_bal.reshape(BLOCKS, TB, KVH, GROUP, HD).transpose(0, 2, 1, 3, 4).reshape(BLOCKS, KVH, TB * GROUP, HD)
    grad_blocks = grad_bal.reshape(BLOCKS, TB, KVH, GROUP, HD).transpose(0, 2, 1, 3, 4).reshape(BLOCKS, KVH, TB * GROUP, HD)
    positions = jnp.arange(KEYS).astype(jnp.int32)
    in_tile = (positions % TOKP) < TILE_TOK

    def visit_block(carry, inputs):
        key_acc, value_acc = carry
        query_heads, grad_heads, owner_id, tile_count = inputs
        key_heads = img_keys[owner_id].reshape(KEYS, KVH, HD).transpose(1, 0, 2)
        value_heads = img_values[owner_id].reshape(KEYS, KVH, HD).transpose(1, 0, 2)
        valid_keys = in_tile & ((positions // TOKP) < tile_count)
        out_part, query_part, key_part, value_part = jax.vmap(head_pass, in_axes=(0, 0, 0, 0, None))(
            query_heads, grad_heads, key_heads, value_heads, valid_keys)
        key_acc = key_acc.at[owner_id].add(key_part.transpose(1, 0, 2).reshape(KEYS, KVH * HD))
        value_acc = value_acc.at[owner_id].add(value_part.transpose(1, 0, 2).reshape(KEYS, KVH * HD))
        return (key_acc, value_acc), (out_part, query_part)

    zero_acc = jnp.zeros((IMAGES, KEYS, KVH * HD), jnp.float32)
    (key_acc, value_acc), (out_all, query_all) = lax.scan(
        visit_block, (zero_acc, zero_acc), (query_blocks, grad_blocks, owners, tile_counts))
    out_rows = out_all.reshape(BLOCKS, KVH, TB, GROUP, HD).transpose(0, 2, 1, 3, 4).reshape(TOKENS, HQ * HD)
    query_rows = query_all.reshape(BLOCKS, KVH, TB, GROUP, HD).transpose(0, 2, 1, 3, 4).reshape(TOKENS, HQ * HD)
    attended = out_rows[place].astype(jnp.bfloat16)
    grad_queries = query_rows[place].astype(jnp.bfloat16)
    return attended, grad_queries, key_acc.astype(jnp.bfloat16), value_acc.astype(jnp.bfloat16)
```

```python
import functools

import jax
import jax.numpy as jnp
from jax import lax
from jax.experimental import pallas as pl
from jax.experimental.pallas import tpu as pltpu
from jax.sharding import PartitionSpec as P

HD = 128
TILE_TOK = 1601
TOKP = 1664
KEYS = 6656
SCALE = HD**-0.5
LOG2E = 1.4426950408889634
RANKS = 32
CHUNKS = 4
WIDTH = 256
SLAB = 16
SLABS = RANKS * SLAB
OWN = 96
FAR = 64
BAL = 2 * (OWN + FAR)
ROWS = 2 * (OWN + FAR)
STEP = 3328
STEPS = KEYS // STEP
MESH = pl.DeviceIdType.MESH
f32 = jnp.float32
bf16 = jnp.bfloat16
NT = ((1,), (1,))
NN = ((1,), (0,))


def dot(a, b, dims=NN):
    return lax.dot_general(a, b, (dims, ((), ())), preferred_element_type=f32)


def iota(shape, dim):
    return lax.broadcasted_iota(jnp.int32, shape, dim)


def fold(x, op):
    r = x[:, :HD]
    for i in range(1, x.shape[1] // HD):
        r = op(r, x[:, i * HD : (i + 1) * HD])
    return r


def as_column(row, n):
    return jnp.transpose(jnp.broadcast_to(row, (HD, n)))[:, :1]


def kernel(
    image_ref, owner_ref, tiles_ref, dest_ref, slot_ref, q_ref, g_ref, k_ref, v_ref,
    att_ref, gq_ref, gk_ref, gv_ref,
    snd, rcv, rep, ret, tab, tab_in, bal, far, res, back,
    pack, unpack, place, unplace, scores, weights, gk_t, gv_t,
    in_send, in_recv, tab_send, tab_recv, far_send, far_recv, back_send, back_recv, out_send, out_recv,
):
    me = lax.axis_index("dp")
    mz, mx = me // 4, me % 4

    def ahead(k):
        return {"dp": ((mz + k // 4) % 8) * 4 + (mx + k % 4) % 4}

    def behind(k):
        return {"dp": ((mz + 8 - k // 4) % 8) * 4 + (mx + 4 - k % 4) % 4}

    nxt = {"dp": (me + 1) % RANKS}
    prv = {"dp": (me + RANKS - 1) % RANKS}
    barrier = pltpu.get_barrier_semaphore()

    @pl.loop(1, RANKS)
    def _(k):
        pl.semaphore_signal(barrier, 1, device_id=ahead(k), device_id_type=MESH)

    dest = dest_ref[...]
    slot = slot_ref[...]
    offset = (((dest >> 2) - mz) & 7) * 4 + (((dest & 3) - mx) & 3)
    dest_c = as_column(dest, HD)
    same = (dest_c == dest) & (iota((HD, HD), 0) < iota((HD, HD), 1))
    position = jnp.sum(same.astype(jnp.int32), axis=0, keepdims=True)
    target = jnp.concatenate([offset * SLAB + position, offset * SLAB + 8 + position], axis=1)
    pack[...] = (iota((SLABS, 2 * HD), 0) == target).astype(bf16)
    unpack[...] = (as_column(target, 2 * HD) == iota((2 * HD, SLABS), 1)).astype(bf16)
    position_c = as_column(position, HD)
    slot_c = as_column(slot, HD)
    which = (iota((RANKS, HD), 0) == offset).astype(bf16)
    named = jnp.where(position_c == (iota((HD, HD), 1) & 7), slot_c + 1, 0).astype(bf16)
    tab[...] = dot(which, named)

    pl.semaphore_wait(barrier, RANKS - 1)

    @pl.loop(1, RANKS)
    def _(k):
        pltpu.make_async_remote_copy(
            tab.at[pl.ds(k, 1)], tab_in.at[pl.ds(k, 1)], tab_send, tab_recv,
            device_id=ahead(k), device_id_type=MESH,
        ).start()

    tab_in[0:1] = tab[0:1]

    def slab(k):
        return pl.ds(pl.multiple_of(k * SLAB, SLAB), SLAB)

    for c in range(CHUNKS):
        cols = pl.ds(c * WIDTH, WIDTH)
        rows = jnp.concatenate([q_ref[:, cols], g_ref[:, cols]], axis=0)
        snd[c] = dot(pack[...], rows).astype(bf16)

        @pl.loop(1, RANKS)
        def _(k, c=c):
            pltpu.make_async_remote_copy(
                snd.at[c, slab(k)], rcv.at[c, slab(k)], in_send.at[c], in_recv.at[c],
                device_id=ahead(k), device_id_type=MESH,
            ).start()

        rcv[c, 0:SLAB] = snd[c, 0:SLAB]

    gk_t[...] = jnp.zeros_like(gk_t)
    gv_t[...] = jnp.zeros_like(gv_t)

    rest = pl.ds(1, RANKS - 1)
    pltpu.make_async_copy(tab.at[rest], tab_in.at[rest], tab_recv).wait()
    pltpu.make_async_copy(tab.at[rest], tab_in.at[rest], tab_send).wait()
    spread = jnp.broadcast_to(tab_in[...][:, None, :], (RANKS, SLAB, HD))
    pick = iota((RANKS, SLAB, HD), 2) == (iota((RANKS, SLAB, HD), 1) & 7)
    got = jnp.sum(jnp.where(pick, spread, 0.0), axis=2, keepdims=True)
    got = got.reshape(SLABS, 1).astype(jnp.int32) - 1
    is_far = [(owner_ref[image_ref[b]] != me).astype(jnp.int32) for b in range(4)]
    seat = jnp.full((SLABS, 1), -1, jnp.int32)
    half = (iota((SLABS, 1), 0) >> 3) & 1
    owns, fars = 0, 0
    for b in range(4):
        own_row = owns * 32 + half * OWN
        far_row = 2 * OWN + fars * 32 + half * FAR
        base = own_row + (far_row - own_row) * is_far[b]
        seat = jnp.where((got >> 5) == b, base + (got & 31), seat)
        fars = fars + is_far[b]
        owns = owns + 1 - is_far[b]
    unplace[...] = (seat == iota((SLABS, BAL), 1)).astype(bf16)
    seat_r = jnp.transpose(jnp.broadcast_to(seat, (SLABS, HD)))[:1]
    place[...] = (iota((BAL, SLABS), 0) == seat_r).astype(bf16)

    all_but_first = pl.ds(SLAB, SLABS - SLAB)
    far_rows = pl.ds(2 * OWN, 2 * FAR)

    def far_copy(c):
        return pltpu.make_async_remote_copy(
            bal.at[c, far_rows], far.at[c], far_send.at[c], far_recv.at[c],
            device_id=nxt, device_id_type=MESH,
        )

    def back_copy(c):
        return pltpu.make_async_remote_copy(
            back.at[c], res.at[c, far_rows], back_send.at[c], back_recv.at[c],
            device_id=prv, device_id_type=MESH,
        )

    def take_in(c):
        pltpu.make_async_copy(snd.at[c, all_but_first], rcv.at[c, all_but_first], in_recv.at[c]).wait()
        bal[c] = dot(place[...], rcv[c]).astype(bf16)
        far_copy(c).start()

    def send_out(c):
        back_copy(c).wait_recv()
        rep[c] = dot(unplace[...], res[c]).astype(bf16)

        @pl.loop(1, RANKS)
        def _(k):
            pltpu.make_async_remote_copy(
                rep.at[c, slab(k)], ret.at[c, slab(k)], out_send.at[c], out_recv.at[c],
                device_id=behind(k), device_id_type=MESH,
            ).start()

        ret[c, 0:SLAB] = rep[c, 0:SLAB]

    def gather_rows(c, own_at, far_at):
        parts = []
        for h in range(2):
            cols = slice(h * HD, (h + 1) * HD)
            parts += [bal[c, own_at : own_at + OWN, cols], far[c, far_at : far_at + FAR, cols]]
        return jnp.concatenate(parts, axis=0)

    def put_rows(c, x, own_at, far_at):
        for h in range(2):
            cols = slice(h * HD, (h + 1) * HD)
            top = h * (OWN + FAR)
            res[c, own_at : own_at + OWN, cols] = x[top : top + OWN]
            back[c, far_at : far_at + FAR, cols] = x[top + OWN : top + OWN + FAR]

    def keys_of(j):
        return pl.ds(pl.multiple_of(j * STEP, STEP), STEP)

    count = tiles_ref[0]
    take_in(0)

    @pl.loop(0, CHUNKS)
    def _(c):
        far_copy(c).wait_recv()
        q = gather_rows(c, 0, 0)
        g = gather_rows(c, OWN, FAR)

        def score_step(j, top):
            s = dot(q, k_ref[0, keys_of(j), :], NT)
            at = iota((1, STEP), 1) + j * STEP
            valid = (at % TOKP < TILE_TOK) & (at // TOKP < count)
            s = s + jnp.where(valid, 0.0, -1e30)
            scores[j] = s
            return jnp.maximum(top, fold(s, jnp.maximum))

        top = lax.fori_loop(0, STEPS, score_step, jnp.full((ROWS, HD), -3e38, f32))
        top = jnp.max(top, axis=1, keepdims=True) * (SCALE * LOG2E)

        def out_step(j, carry):
            total, out = carry
            e = jnp.exp2(scores[j] * (SCALE * LOG2E) - top)
            low = e.astype(bf16)
            weights[j] = low
            return total + fold(e, jnp.add), out + dot(low, v_ref[0, keys_of(j), :])

        zeros = jnp.zeros((ROWS, HD), f32)
        total, out = lax.fori_loop(0, STEPS, out_step, (zeros, zeros))
        inverse = 1.0 / jnp.sum(total, axis=1, keepdims=True)
        out = out * inverse
        put_rows(c, out.astype(bf16), 0, 0)

        @pl.when(c > 0)
        def _():
            send_out(c - 1)

        @pl.when(c < CHUNKS - 1)
        def _():
            take_in(c + 1)

        g32 = g.astype(f32)
        delta = jnp.sum(g32 * out, axis=1, keepdims=True)
        g_t = jnp.transpose(g32 * inverse).astype(bf16)
        q_t = jnp.transpose(q.astype(f32) * (inverse * SCALE)).astype(bf16)

        def grad_step(j, grad_q):
            dp = dot(g, v_ref[0, keys_of(j), :], NT)
            low = weights[j]
            ds = (low.astype(f32) * (dp - delta)).astype(bf16)
            gv_t[j] += dot(g_t, low)
            gk_t[j] += dot(q_t, ds)
            return grad_q + dot(ds, k_ref[0, keys_of(j), :])

        grad_q = lax.fori_loop(0, STEPS, grad_step, zeros)
        put_rows(c, (grad_q * (inverse * SCALE)).astype(bf16), OWN, FAR)
        back_copy(c).start()

    send_out(CHUNKS - 1)

    for j in range(STEPS):
        gk_ref[0, j * STEP : (j + 1) * STEP] = jnp.transpose(gk_t[j]).astype(bf16)
        gv_ref[0, j * STEP : (j + 1) * STEP] = jnp.transpose(gv_t[j]).astype(bf16)

    for c in range(CHUNKS):
        pltpu.make_async_copy(rep.at[c, all_but_first], ret.at[c, all_but_first], out_recv.at[c]).wait()
        final = dot(unpack[...], ret[c]).astype(bf16)
        cols = slice(c * WIDTH, (c + 1) * WIDTH)
        att_ref[:, cols] = final[:HD]
        gq_ref[:, cols] = final[HD:]

    for c in range(CHUNKS):
        pltpu.make_async_copy(snd.at[c, all_but_first], rcv.at[c, all_but_first], in_send.at[c]).wait()
        pltpu.make_async_copy(rep.at[c, all_but_first], ret.at[c, all_but_first], out_send.at[c]).wait()
        far_copy(c).wait_send()
        back_copy(c).wait_send()


def shards(queries, grad_out, row_dest, row_slot, block_image, image_owner, image_tiles, img_keys, img_values):
    vmem = pl.BlockSpec(memory_space=pltpu.VMEM)
    smem = pl.BlockSpec(memory_space=pltpu.SMEM)
    dma = pltpu.SemaphoreType.DMA
    slabs = pltpu.VMEM((CHUNKS, SLABS, WIDTH), bf16)
    return pl.pallas_call(
        kernel,
        out_shape=(
            jax.ShapeDtypeStruct(queries.shape, bf16),
            jax.ShapeDtypeStruct(queries.shape, bf16),
            jax.ShapeDtypeStruct(img_keys.shape, bf16),
            jax.ShapeDtypeStruct(img_keys.shape, bf16),
        ),
        in_specs=[smem] * 3 + [vmem] * 6,
        out_specs=(vmem,) * 4,
        scratch_shapes=[
            slabs, slabs, slabs, slabs,
            pltpu.VMEM((RANKS, HD), f32),
            pltpu.VMEM((RANKS, HD), f32),
            pltpu.VMEM((CHUNKS, BAL, WIDTH), bf16),
            pltpu.VMEM((CHUNKS, 2 * FAR, WIDTH), bf16),
            pltpu.VMEM((CHUNKS, BAL, WIDTH), bf16),
            pltpu.VMEM((CHUNKS, 2 * FAR, WIDTH), bf16),
            pltpu.VMEM((SLABS, 2 * HD), bf16),
            pltpu.VMEM((2 * HD, SLABS), bf16),
            pltpu.VMEM((BAL, SLABS), bf16),
            pltpu.VMEM((SLABS, BAL), bf16),
            pltpu.VMEM((STEPS, ROWS, STEP), f32),
            pltpu.VMEM((STEPS, ROWS, STEP), bf16),
            pltpu.VMEM((STEPS, HD, STEP), f32),
            pltpu.VMEM((STEPS, HD, STEP), f32),
            dma((CHUNKS,)), dma((CHUNKS,)), dma, dma,
            dma((CHUNKS,)), dma((CHUNKS,)), dma((CHUNKS,)), dma((CHUNKS,)),
            dma((CHUNKS,)), dma((CHUNKS,)),
        ],
        compiler_params=pltpu.CompilerParams(
            collective_id=0, has_side_effects=True, vmem_limit_bytes=56 * 1024 * 1024
        ),
    )(
        block_image, image_owner, image_tiles, row_dest.reshape(1, -1), row_slot.reshape(1, -1),
        queries, grad_out, img_keys, img_values,
    )


def solution(mesh):
    return jax.shard_map(
        shards,
        mesh=mesh,
        in_specs=(
            P("dp", "mp"),
            P("dp", "mp"),
            P("dp"),
            P("dp"),
            P("dp"),
            P(),
            P("dp"),
            P("dp", None, "mp"),
            P("dp", None, "mp"),
        ),
        out_specs=(P("dp", "mp"), P("dp", "mp"), P("dp", None, "mp"), P("dp", None, "mp")),
        check_vma=False,
    )
```

```python
import functools

import jax
import jax.numpy as jnp
from jax import lax
from jax.experimental import pallas as pl
from jax.experimental.pallas import tpu as pltpu
from jax.sharding import PartitionSpec as P

HD = 128
TILE_TOK = 1601
TOKP = 1664
KEYS = 6656
SCALE = HD**-0.5
LOG2E = 1.4426950408889634
RANKS = 32
CHUNKS = 4
WIDTH = 256
SLAB = 16
SLABS = RANKS * SLAB
OWN = 96
FAR = 64
BAL = 2 * (OWN + FAR)
ROWS = 2 * (OWN + FAR)
STEP = 3328
STEPS = KEYS // STEP
AHEAD = 2
PARTS = 4
MESH = pl.DeviceIdType.MESH
f32 = jnp.float32
bf16 = jnp.bfloat16
NT = ((1,), (1,))
NN = ((1,), (0,))


def dot(a, b, dims=NN):
    return lax.dot_general(a, b, (dims, ((), ())), preferred_element_type=f32)


def iota(shape, dim):
    return lax.broadcasted_iota(jnp.int32, shape, dim)


def fold(x, op):
    r = x[:, :HD]
    for i in range(1, x.shape[1] // HD):
        r = op(r, x[:, i * HD : (i + 1) * HD])
    return r


def as_column(row, n):
    return jnp.transpose(jnp.broadcast_to(row, (HD, n)))[:, :1]


def kernel(
    image_ref, owner_ref, tiles_ref, dest_ref, slot_ref, q_ref, g_ref, k_ref, v_ref,
    att_ref, gq_ref, gk_ref, gv_ref,
    snd, rcv, rep, ret, tab, tab_in, bal, far, res, back,
    pack, unpack, place, unplace, scores, weights, slopes, q_low, g_low, k_buf, v_buf,
    held, in_send, in_recv, tab_send, tab_recv, far_send, far_recv, back_send, back_recv, out_send, out_recv,
):
    me = lax.axis_index("dp")
    mz, mx = me // 4, me % 4

    def ahead(k):
        return {"dp": ((mz + k // 4) % 8) * 4 + (mx + k % 4) % 4}

    def behind(k):
        return {"dp": ((mz + 8 - k // 4) % 8) * 4 + (mx + 4 - k % 4) % 4}

    nxt = {"dp": (me + 1) % RANKS}
    prv = {"dp": (me + RANKS - 1) % RANKS}
    barrier = pltpu.get_barrier_semaphore()
    get_k = pltpu.make_async_copy(k_ref.at[0], k_buf, held.at[0])
    get_v = pltpu.make_async_copy(v_ref.at[0], v_buf, held.at[1])
    put_k = pltpu.make_async_copy(k_buf, gk_ref.at[0], held.at[0])
    put_v = pltpu.make_async_copy(v_buf, gv_ref.at[0], held.at[1])
    get_k.start()
    get_v.start()

    @pl.loop(1, RANKS)
    def _(k):
        pl.semaphore_signal(barrier, 1, device_id=ahead(k), device_id_type=MESH)

    dest = dest_ref[...]
    slot = slot_ref[...]
    offset = (((dest >> 2) - mz) & 7) * 4 + (((dest & 3) - mx) & 3)
    dest_c = as_column(dest, HD)
    same = (dest_c == dest) & (iota((HD, HD), 0) < iota((HD, HD), 1))
    position = jnp.sum(same.astype(jnp.int32), axis=0, keepdims=True)
    target = jnp.concatenate([offset * SLAB + position, offset * SLAB + 8 + position], axis=1)
    pack[...] = (iota((SLABS, 2 * HD), 0) == target).astype(bf16)
    unpack[...] = (as_column(target, 2 * HD) == iota((2 * HD, SLABS), 1)).astype(bf16)
    position_c = as_column(position, HD)
    slot_c = as_column(slot, HD)
    which = (iota((RANKS, HD), 0) == offset).astype(bf16)
    named = jnp.where(position_c == (iota((HD, HD), 1) & 7), slot_c + 1, 0).astype(bf16)
    tab[...] = dot(which, named)

    for c in range(CHUNKS):
        cols = slice(c * WIDTH, (c + 1) * WIDTH)
        rows = jnp.concatenate([q_ref[:, cols], g_ref[:, cols]], axis=0)
        snd[c] = dot(pack[...], rows).astype(bf16)
        rcv[c, 0:SLAB] = snd[c, 0:SLAB]
    tab_in[0:1] = tab[0:1]

    pl.semaphore_wait(barrier, RANKS - 1)

    @pl.loop(1, RANKS)
    def _(k):
        pltpu.make_async_remote_copy(
            tab.at[pl.ds(k, 1)], tab_in.at[pl.ds(k, 1)], tab_send, tab_recv,
            device_id=ahead(k), device_id_type=MESH,
        ).start()

    def slab(k):
        return pl.ds(pl.multiple_of(k * SLAB, SLAB), SLAB)

    def send_in(c):
        @pl.loop(1, RANKS)
        def _(k):
            pltpu.make_async_remote_copy(
                snd.at[c, slab(k)], rcv.at[c, slab(k)], in_send.at[c], in_recv.at[c],
                device_id=ahead(k), device_id_type=MESH,
            ).start()

    for c in range(AHEAD):
        send_in(c)

    rest = pl.ds(1, RANKS - 1)
    pltpu.make_async_copy(tab.at[rest], tab_in.at[rest], tab_recv).wait()
    pltpu.make_async_copy(tab.at[rest], tab_in.at[rest], tab_send).wait()
    spread = jnp.broadcast_to(tab_in[...][:, None, :], (RANKS, SLAB, HD))
    pick = iota((RANKS, SLAB, HD), 2) == (iota((RANKS, SLAB, HD), 1) & 7)
    got = jnp.sum(jnp.where(pick, spread, 0.0), axis=2, keepdims=True)
    got = got.reshape(SLABS, 1).astype(jnp.int32) - 1
    is_far = [(owner_ref[image_ref[b]] != me).astype(jnp.int32) for b in range(4)]
    seat = jnp.full((SLABS, 1), -1, jnp.int32)
    half = (iota((SLABS, 1), 0) >> 3) & 1
    owns, fars = 0, 0
    for b in range(4):
        own_row = owns * 32 + half * OWN
        far_row = 2 * OWN + fars * 32 + half * FAR
        base = own_row + (far_row - own_row) * is_far[b]
        seat = jnp.where((got >> 5) == b, base + (got & 31), seat)
        fars = fars + is_far[b]
        owns = owns + 1 - is_far[b]
    unplace[...] = (seat == iota((SLABS, BAL), 1)).astype(bf16)
    seat_r = jnp.transpose(jnp.broadcast_to(seat, (SLABS, HD)))[:1]
    place[...] = (iota((BAL, SLABS), 0) == seat_r).astype(bf16)

    all_but_first = pl.ds(SLAB, SLABS - SLAB)
    far_rows = pl.ds(2 * OWN, 2 * FAR)

    def far_copy(c):
        return pltpu.make_async_remote_copy(
            bal.at[c, far_rows], far.at[c], far_send.at[c], far_recv.at[c],
            device_id=nxt, device_id_type=MESH,
        )

    def back_copy(c):
        return pltpu.make_async_remote_copy(
            back.at[c], res.at[c, far_rows], back_send.at[c], back_recv.at[c],
            device_id=prv, device_id_type=MESH,
        )

    def take_in(c):
        pltpu.make_async_copy(snd.at[c, all_but_first], rcv.at[c, all_but_first], in_recv.at[c]).wait()
        bal[c, 2 * OWN :] = dot(place[2 * OWN :], rcv[c]).astype(bf16)
        far_copy(c).start()

        @pl.when(c + AHEAD < CHUNKS)
        def _():
            send_in(c + AHEAD)

        bal[c, : 2 * OWN] = dot(place[: 2 * OWN], rcv[c]).astype(bf16)

    def send_out(c):
        back_copy(c).wait_recv()
        rep[c] = dot(unplace[...], res[c]).astype(bf16)

        @pl.loop(1, RANKS)
        def _(k):
            pltpu.make_async_remote_copy(
                rep.at[c, slab(k)], ret.at[c, slab(k)], out_send.at[c], out_recv.at[c],
                device_id=behind(k), device_id_type=MESH,
            ).start()

        ret[c, 0:SLAB] = rep[c, 0:SLAB]

    def gather_rows(c, own_at, far_at):
        parts = []
        for h in range(2):
            cols = slice(h * HD, (h + 1) * HD)
            parts += [bal[c, own_at : own_at + OWN, cols], far[c, far_at : far_at + FAR, cols]]
        return jnp.concatenate(parts, axis=0)

    def put_rows(c, x, own_at, far_at):
        for h in range(2):
            cols = slice(h * HD, (h + 1) * HD)
            top = h * (OWN + FAR)
            res[c, own_at : own_at + OWN, cols] = x[top : top + OWN]
            back[c, far_at : far_at + FAR, cols] = x[top + OWN : top + OWN + FAR]

    def keys_of(j):
        return pl.ds(pl.multiple_of(j * STEP, STEP), STEP)

    count = tiles_ref[0]
    take_in(0)
    get_k.wait()
    get_v.wait()

    @pl.loop(0, CHUNKS)
    def _(c):
        pairs = pl.ds(pl.multiple_of(c * ROWS, ROWS), ROWS)
        far_copy(c).wait_recv()
        q = gather_rows(c, 0, 0)
        g = gather_rows(c, OWN, FAR)

        def score_step(j, top):
            s = dot(q, k_buf[keys_of(j), :], NT)
            at = iota((1, STEP), 1) + j * STEP
            valid = (at % TOKP < TILE_TOK) & (at // TOKP < count)
            s = s + jnp.where(valid, 0.0, -1e30)
            scores[j] = s
            return jnp.maximum(top, fold(s, jnp.maximum))

        top = lax.fori_loop(0, STEPS, score_step, jnp.full((ROWS, HD), -3e38, f32))
        top = jnp.max(top, axis=1, keepdims=True) * (SCALE * LOG2E)

        @pl.when(c < CHUNKS - 1)
        def _():
            take_in(c + 1)

        def out_step(j, carry):
            total, out = carry
            e = jnp.exp2(scores[j] * (SCALE * LOG2E) - top)
            low = e.astype(bf16)
            weights[j, pairs] = low
            return total + fold(e, jnp.add), out + dot(low, v_buf[keys_of(j), :])

        zeros = jnp.zeros((ROWS, HD), f32)
        total, out = lax.fori_loop(0, STEPS, out_step, (zeros, zeros))
        inverse = 1.0 / jnp.sum(total, axis=1, keepdims=True)
        out = out * inverse
        put_rows(c, out.astype(bf16), 0, 0)

        g32 = g.astype(f32)
        delta = jnp.sum(g32 * out, axis=1, keepdims=True)
        g_low[pairs] = (g32 * inverse).astype(bf16)
        q_low[pairs] = (q.astype(f32) * (inverse * SCALE)).astype(bf16)

        def grad_step(j, grad_q):
            dp = dot(g, v_buf[keys_of(j), :], NT)
            ds = (weights[j, pairs].astype(f32) * (dp - delta)).astype(bf16)
            slopes[j, pairs] = ds
            return grad_q + dot(ds, k_buf[keys_of(j), :])

        grad_q = lax.fori_loop(0, STEPS, grad_step, zeros)
        put_rows(c, (grad_q * (inverse * SCALE)).astype(bf16), OWN, FAR)
        back_copy(c).start()

        @pl.when(c > 0)
        def _():
            send_out(c - 1)

    g_t = jnp.transpose(g_low[...].astype(f32)).astype(bf16)
    q_t = jnp.transpose(q_low[...].astype(f32)).astype(bf16)
    k_buf[0:STEP] = jnp.transpose(dot(q_t, slopes[0])).astype(bf16)
    send_out(CHUNKS - 1)
    for j in range(STEPS):
        mine = slice(j * STEP, (j + 1) * STEP)
        v_buf[mine] = jnp.transpose(dot(g_t, weights[j])).astype(bf16)
        if j:
            k_buf[mine] = jnp.transpose(dot(q_t, slopes[j])).astype(bf16)
    put_k.start()
    put_v.start()

    for c in range(CHUNKS):
        pltpu.make_async_copy(rep.at[c, all_but_first], ret.at[c, all_but_first], out_recv.at[c]).wait()
        final = dot(unpack[...], ret[c]).astype(bf16)
        cols = slice(c * WIDTH, (c + 1) * WIDTH)
        att_ref[:, cols] = final[:HD]
        gq_ref[:, cols] = final[HD:]

    for c in range(CHUNKS):
        pltpu.make_async_copy(snd.at[c, all_but_first], rcv.at[c, all_but_first], in_send.at[c]).wait()
        pltpu.make_async_copy(rep.at[c, all_but_first], ret.at[c, all_but_first], out_send.at[c]).wait()
        far_copy(c).wait_send()
        back_copy(c).wait_send()
    put_k.wait()
    put_v.wait()


def finish(*refs):
    sems = refs[-1]
    moves = []
    for a, (src, dst, via) in enumerate(zip(refs[:4], refs[4:8], refs[8:12])):
        axis = src.shape.index(max(src.shape))
        part = src.shape[axis] // PARTS
        for p in range(PARTS):
            at = (slice(None),) * axis + (pl.ds(p * part, part),)
            moves.append((
                pltpu.make_async_copy(src.at[at], via.at[at], sems.at[0, a, p]),
                pltpu.make_async_copy(via.at[at], dst.at[at], sems.at[1, a, p]),
            ))
    for come, _ in moves:
        come.start()
    for come, go in moves:
        come.wait()
        go.start()
    for _, go in moves:
        go.wait()


def shards(queries, grad_out, row_dest, row_slot, block_image, image_owner, image_tiles, img_keys, img_values):
    vmem = pl.BlockSpec(memory_space=pltpu.VMEM)
    smem = pl.BlockSpec(memory_space=pltpu.SMEM)
    hbm = pl.BlockSpec(memory_space=pl.ANY)
    dma = pltpu.SemaphoreType.DMA
    slabs = pltpu.VMEM((CHUNKS, SLABS, WIDTH), bf16)
    shapes = tuple(jax.ShapeDtypeStruct(x.shape, bf16) for x in (queries, grad_out, img_keys, img_values))
    results = pl.pallas_call(
        kernel,
        out_shape=shapes,
        in_specs=[smem] * 3 + [vmem] * 4 + [hbm] * 2,
        out_specs=(vmem, vmem, hbm, hbm),
        scratch_shapes=[
            slabs, slabs, slabs, slabs,
            pltpu.VMEM((RANKS, HD), f32),
            pltpu.VMEM((RANKS, HD), f32),
            pltpu.VMEM((CHUNKS, BAL, WIDTH), bf16),
            pltpu.VMEM((CHUNKS, 2 * FAR, WIDTH), bf16),
            pltpu.VMEM((CHUNKS, BAL, WIDTH), bf16),
            pltpu.VMEM((CHUNKS, 2 * FAR, WIDTH), bf16),
            pltpu.VMEM((SLABS, 2 * HD), bf16),
            pltpu.VMEM((2 * HD, SLABS), bf16),
            pltpu.VMEM((BAL, SLABS), bf16),
            pltpu.VMEM((SLABS, BAL), bf16),
            pltpu.VMEM((STEPS, ROWS, STEP), f32),
            pltpu.VMEM((STEPS, CHUNKS * ROWS, STEP), bf16),
            pltpu.VMEM((STEPS, CHUNKS * ROWS, STEP), bf16),
            pltpu.VMEM((CHUNKS * ROWS, HD), bf16),
            pltpu.VMEM((CHUNKS * ROWS, HD), bf16),
            pltpu.VMEM((KEYS, HD), bf16),
            pltpu.VMEM((KEYS, HD), bf16),
            dma((2,)),
            dma((CHUNKS,)), dma((CHUNKS,)), dma, dma,
            dma((CHUNKS,)), dma((CHUNKS,)), dma((CHUNKS,)), dma((CHUNKS,)),
            dma((CHUNKS,)), dma((CHUNKS,)),
        ],
        compiler_params=pltpu.CompilerParams(
            collective_id=0, has_side_effects=True, vmem_limit_bytes=62 * 1024 * 1024
        ),
    )(
        block_image, image_owner, image_tiles, row_dest.reshape(1, -1), row_slot.reshape(1, -1),
        queries, grad_out, img_keys, img_values,
    )
    return pl.pallas_call(
        finish,
        out_shape=shapes,
        in_specs=[hbm] * 4,
        out_specs=(hbm,) * 4,
        scratch_shapes=[pltpu.VMEM(x.shape, bf16) for x in shapes] + [dma((2, 4, PARTS))],
        compiler_params=pltpu.CompilerParams(vmem_limit_bytes=62 * 1024 * 1024),
    )(*results)


def solution(mesh):
    return jax.shard_map(
        shards,
        mesh=mesh,
        in_specs=(
            P("dp", "mp"),
            P("dp", "mp"),
            P("dp"),
            P("dp"),
            P("dp"),
            P(),
            P("dp"),
            P("dp", None, "mp"),
            P("dp", None, "mp"),
        ),
        out_specs=(P("dp", "mp"), P("dp", "mp"), P("dp", None, "mp"), P("dp", None, "mp")),
        check_vma=False,
    )
```

```python
import functools

import jax
import jax.numpy as jnp
from jax import lax
from jax.experimental import pallas as pl
from jax.experimental.pallas import tpu as pltpu
from jax.sharding import PartitionSpec as P

HD = 128
TILE_TOK = 1601
TOKP = 1664
KEYS = 6656
SCALE = HD**-0.5
LOG2E = 1.4426950408889634
RANKS = 32
CHUNKS = 4
WIDTH = 256
SLAB = 16
SLABS = RANKS * SLAB
OWN = 96
FAR = 64
BAL = 2 * (OWN + FAR)
ROWS = 2 * (OWN + FAR)
STEP = 3328
STEPS = KEYS // STEP
AHEAD = 2
MESH = pl.DeviceIdType.MESH
f32 = jnp.float32
bf16 = jnp.bfloat16
NT = ((1,), (1,))
NN = ((1,), (0,))


def dot(a, b, dims=NN):
    return lax.dot_general(a, b, (dims, ((), ())), preferred_element_type=f32)


def iota(shape, dim):
    return lax.broadcasted_iota(jnp.int32, shape, dim)


def fold(x, op):
    r = x[:, :HD]
    for i in range(1, x.shape[1] // HD):
        r = op(r, x[:, i * HD : (i + 1) * HD])
    return r


def as_column(row, n):
    return jnp.transpose(jnp.broadcast_to(row, (HD, n)))[:, :1]


def kernel(
    image_ref, owner_ref, tiles_ref, dest_ref, slot_ref, q_ref, g_ref, k_ref, v_ref,
    att_ref, gq_ref, k_buf, v_buf,
    snd, rcv, rep, ret, tab, tab_in, bal, far, res, back,
    pack, unpack, place, unplace, scores, weights, slopes, q_low, g_low, rows,
    entered, held, in_send, in_recv, tab_send, tab_recv, far_send, far_recv, back_send, back_recv, out_send, out_recv,
):
    me = lax.axis_index("dp")
    mz, mx = me >> 2, me & 3

    def ahead(k):
        return {"dp": ((mz + (k >> 2)) & 7) * 4 + ((mx + (k & 3)) & 3)}

    def behind(k):
        return {"dp": ((mz + 8 - (k >> 2)) & 7) * 4 + ((mx + 4 - (k & 3)) & 3)}

    def to_all(send):
        for k in range(1, 4):
            send(k)

        @pl.loop(1, 8)
        def _(dz):
            for dx in range(4):
                send(dz * 4 + dx)

    nxt = {"dp": (me + 1) & (RANKS - 1)}
    prv = {"dp": (me + RANKS - 1) & (RANKS - 1)}
    barrier = pltpu.get_barrier_semaphore()
    get_k = pltpu.make_async_copy(k_ref, k_buf, held.at[0])
    get_v = pltpu.make_async_copy(v_ref, v_buf, held.at[1])
    get_q = pltpu.make_async_copy(q_ref, rows.at[pl.ds(0, HD)], held.at[2])
    get_g = pltpu.make_async_copy(g_ref, rows.at[pl.ds(HD, HD)], held.at[3])
    get_q.start()
    get_g.start()
    get_k.start()
    get_v.start()

    lines = [k for k in range(1, RANKS) if k < 4 or k % 4 == 0]
    for k in lines:
        pl.semaphore_signal(barrier, 1, device_id=ahead(k), device_id_type=MESH)

    dest = dest_ref[...]
    slot = slot_ref[...]
    offset = (((dest >> 2) - mz) & 7) * 4 + (((dest & 3) - mx) & 3)
    dest_c = as_column(dest, HD)
    same = (dest_c == dest) & (iota((HD, HD), 0) < iota((HD, HD), 1))
    position = jnp.sum(same.astype(jnp.int32), axis=0, keepdims=True)
    target = jnp.concatenate([offset * SLAB + position, offset * SLAB + 8 + position], axis=1)
    pack[...] = (iota((SLABS, 2 * HD), 0) == target).astype(bf16)
    position_c = as_column(position, HD)
    slot_c = as_column(slot, HD)
    which = (iota((RANKS, HD), 0) == offset).astype(bf16)
    named = jnp.where(position_c == (iota((HD, HD), 1) & 7), slot_c + 1, 0).astype(bf16)
    tab[...] = dot(which, named)

    def fill(c):
        cols = slice(c * WIDTH, (c + 1) * WIDTH)
        snd[c] = dot(pack[...], rows[:, cols]).astype(bf16)
        rcv[c, 0:SLAB] = snd[c, 0:SLAB]

    get_q.wait()
    get_g.wait()
    fill(0)
    tab_in[0:1] = tab[0:1]
    pl.semaphore_wait(barrier, len(lines))
    for k in range(1, 4):
        pl.semaphore_signal(entered, 1, device_id=ahead(k), device_id_type=MESH)
    pl.semaphore_wait(entered, 3)

    def slab(k):
        return pl.ds(k * SLAB if isinstance(k, int) else pl.multiple_of(k * SLAB, SLAB), SLAB)

    def send_in(c):
        def one(k):
            pltpu.make_async_remote_copy(
                snd.at[c, slab(k)], rcv.at[c, slab(k)], in_send.at[c], in_recv.at[c],
                device_id=ahead(k), device_id_type=MESH,
            ).start()

        to_all(one)

    send_in(0)
    def one(k):
        pltpu.make_async_remote_copy(
            tab.at[pl.ds(k, 1)], tab_in.at[pl.ds(k, 1)], tab_send, tab_recv,
            device_id=ahead(k), device_id_type=MESH,
        ).start()

    to_all(one)
    for c in range(1, AHEAD):
        fill(c)
        send_in(c)
    for c in range(AHEAD, CHUNKS):
        fill(c)
    unpack[...] = (as_column(target, 2 * HD) == iota((2 * HD, SLABS), 1)).astype(bf16)

    rest = pl.ds(1, RANKS - 1)
    pltpu.make_async_copy(tab.at[rest], tab_in.at[rest], tab_recv).wait()
    pltpu.make_async_copy(tab.at[rest], tab_in.at[rest], tab_send).wait()
    spread = jnp.broadcast_to(tab_in[...][:, None, :], (RANKS, SLAB, HD))
    pick = iota((RANKS, SLAB, HD), 2) == (iota((RANKS, SLAB, HD), 1) & 7)
    got = jnp.sum(jnp.where(pick, spread, 0.0), axis=2, keepdims=True)
    got = got.reshape(SLABS, 1).astype(jnp.int32) - 1
    is_far = [(owner_ref[image_ref[b]] != me).astype(jnp.int32) for b in range(4)]
    seat = jnp.full((SLABS, 1), -1, jnp.int32)
    half = (iota((SLABS, 1), 0) >> 3) & 1
    owns, fars = 0, 0
    for b in range(4):
        own_row = owns * 32 + half * OWN
        far_row = 2 * OWN + fars * 32 + half * FAR
        base = own_row + (far_row - own_row) * is_far[b]
        seat = jnp.where((got >> 5) == b, base + (got & 31), seat)
        fars = fars + is_far[b]
        owns = owns + 1 - is_far[b]
    unplace[...] = (seat == iota((SLABS, BAL), 1)).astype(bf16)
    seat_r = jnp.transpose(jnp.broadcast_to(seat, (SLABS, HD)))[:1]
    place[...] = (iota((BAL, SLABS), 0) == seat_r).astype(bf16)

    all_but_first = pl.ds(SLAB, SLABS - SLAB)
    far_rows = pl.ds(2 * OWN, 2 * FAR)

    def far_copy(c):
        return pltpu.make_async_remote_copy(
            bal.at[c, far_rows], far.at[c], far_send.at[c], far_recv.at[c],
            device_id=nxt, device_id_type=MESH,
        )

    def back_copy(c):
        return pltpu.make_async_remote_copy(
            back.at[c], res.at[c, far_rows], back_send.at[c], back_recv.at[c],
            device_id=prv, device_id_type=MESH,
        )

    def take_in(c):
        pltpu.make_async_copy(snd.at[c, all_but_first], rcv.at[c, all_but_first], in_recv.at[c]).wait()
        bal[c, 2 * OWN :] = dot(place[2 * OWN :], rcv[c]).astype(bf16)
        far_copy(c).start()

        if isinstance(c, int):
            if c + AHEAD < CHUNKS:
                send_in(c + AHEAD)
        else:

            @pl.when(c + AHEAD < CHUNKS)
            def _():
                send_in(c + AHEAD)

        bal[c, : 2 * OWN] = dot(place[: 2 * OWN], rcv[c]).astype(bf16)

    def send_out(c):
        back_copy(c).wait_recv()
        rep[c] = dot(unplace[...], res[c]).astype(bf16)

        def one(k):
            pltpu.make_async_remote_copy(
                rep.at[c, slab(k)], ret.at[c, slab(k)], out_send.at[c], out_recv.at[c],
                device_id=behind(k), device_id_type=MESH,
            ).start()

        to_all(one)

        ret[c, 0:SLAB] = rep[c, 0:SLAB]

    def segments(group):
        own = [(bal, res, 0, OWN, OWN, h) for h in range(2)]
        away = [(far, back, 0, FAR, FAR, h) for h in range(2)]
        return {"own": own, "far": away, "all": own + away}[group]

    def gather_rows(c, group, second):
        parts = []
        for src, _, first, other, n, h in segments(group):
            at = other if second else first
            parts.append(src[c, at : at + n, h * HD : (h + 1) * HD])
        return jnp.concatenate(parts, axis=0)

    def put_rows(c, group, second, x):
        top = 0
        for _, dst, first, other, n, h in segments(group):
            at = other if second else first
            dst[c, at : at + n, h * HD : (h + 1) * HD] = x[top : top + n]
            top += n

    def keys_of(j):
        return pl.ds(pl.multiple_of(j * STEP, STEP), STEP)

    count = tiles_ref[0]
    take_in(0)
    get_k.wait()
    get_v.wait()

    def attend(c, group, between=None):
        low_at = 2 * OWN if group == "far" else 0
        n = {"own": 2 * OWN, "far": 2 * FAR, "all": ROWS}[group]
        pairs = pl.ds(pl.multiple_of(c * ROWS + low_at, 64), n)
        q = gather_rows(c, group, False)
        g = gather_rows(c, group, True)

        def score_step(j, top):
            s = dot(q, k_buf[0, keys_of(j), :], NT)
            at = iota((1, STEP), 1) + j * STEP
            valid = (at % TOKP < TILE_TOK) & (at // TOKP < count)
            s = s + jnp.where(valid, 0.0, -1e30)
            scores[j, :n] = s
            return jnp.maximum(top, fold(s, jnp.maximum))

        top = lax.fori_loop(0, STEPS, score_step, jnp.full((n, HD), -3e38, f32))
        top = jnp.max(top, axis=1, keepdims=True) * (SCALE * LOG2E)
        if between is not None:
            between()

        def out_step(j, carry):
            total, out = carry
            e = jnp.exp2(scores[j, :n] * (SCALE * LOG2E) - top)
            low = e.astype(bf16)
            weights[j, pairs] = low
            return total + fold(e, jnp.add), out + dot(low, v_buf[0, keys_of(j), :])

        zeros = jnp.zeros((n, HD), f32)
        total, out = lax.fori_loop(0, STEPS, out_step, (zeros, zeros))
        inverse = 1.0 / jnp.sum(total, axis=1, keepdims=True)
        out = out * inverse
        put_rows(c, group, False, out.astype(bf16))
        g32 = g.astype(f32)
        delta = jnp.sum(g32 * out, axis=1, keepdims=True)
        g_low[pairs] = (g32 * inverse).astype(bf16)
        q_low[pairs] = (q.astype(f32) * (inverse * SCALE)).astype(bf16)

        def grad_step(j, grad_q):
            dp = dot(g, v_buf[0, keys_of(j), :], NT)
            ds = (weights[j, pairs].astype(f32) * (dp - delta)).astype(bf16)
            slopes[j, pairs] = ds
            return grad_q + dot(ds, k_buf[0, keys_of(j), :])

        grad_q = lax.fori_loop(0, STEPS, grad_step, zeros)
        put_rows(c, group, True, (grad_q * (inverse * SCALE)).astype(bf16))

    attend(0, "own")
    far_copy(0).wait_recv()
    attend(0, "far", lambda: take_in(1))
    back_copy(0).start()

    @pl.loop(1, CHUNKS)
    def _(c):
        far_copy(c).wait_recv()

        def between():
            @pl.when(c < CHUNKS - 1)
            def _():
                take_in(c + 1)

        attend(c, "all", between)
        back_copy(c).start()
        send_out(c - 1)

    g_t = jnp.transpose(g_low[...].astype(f32)).astype(bf16)
    q_t = jnp.transpose(q_low[...].astype(f32)).astype(bf16)
    for j in range(STEPS):
        mine = slice(j * STEP, (j + 1) * STEP)
        k_buf[0, mine] = jnp.transpose(dot(q_t, slopes[j])).astype(bf16)
        v_buf[0, mine] = jnp.transpose(dot(g_t, weights[j])).astype(bf16)
        if j == 0:
            send_out(CHUNKS - 1)

    for c in range(CHUNKS):
        pltpu.make_async_copy(rep.at[c, all_but_first], ret.at[c, all_but_first], out_recv.at[c]).wait()
        final = dot(unpack[...], ret[c]).astype(bf16)
        cols = slice(c * WIDTH, (c + 1) * WIDTH)
        att_ref[:, cols] = final[:HD]
        gq_ref[:, cols] = final[HD:]

    for c in range(CHUNKS):
        pltpu.make_async_copy(snd.at[c, all_but_first], rcv.at[c, all_but_first], in_send.at[c]).wait()
        pltpu.make_async_copy(rep.at[c, all_but_first], ret.at[c, all_but_first], out_send.at[c]).wait()
        far_copy(c).wait_send()
        back_copy(c).wait_send()


def finish(*refs):
    copies = [
        pltpu.make_async_copy(src, dst, refs[-1].at[i])
        for i, (src, dst) in enumerate(zip(refs[:4], refs[4:8]))
    ]
    for copy in copies:
        copy.start()
    for copy in copies:
        copy.wait()


def shards(queries, grad_out, row_dest, row_slot, block_image, image_owner, image_tiles, img_keys, img_values):
    vmem = pl.BlockSpec(memory_space=pltpu.VMEM)
    smem = pl.BlockSpec(memory_space=pltpu.SMEM)
    hbm = pl.BlockSpec(memory_space=pl.ANY)
    dma = pltpu.SemaphoreType.DMA
    slabs = pltpu.VMEM((CHUNKS, SLABS, WIDTH), bf16)
    shapes = tuple(jax.ShapeDtypeStruct(x.shape, bf16) for x in (queries, grad_out, img_keys, img_values))
    results = pl.pallas_call(
        kernel,
        out_shape=tuple(pltpu.VMEM(x.shape, bf16) for x in shapes),
        in_specs=[smem] * 3 + [vmem] * 2 + [hbm] * 4,
        out_specs=(vmem,) * 4,
        scratch_shapes=[
            slabs, slabs, slabs, slabs,
            pltpu.VMEM((RANKS, HD), f32),
            pltpu.VMEM((RANKS, HD), f32),
            pltpu.VMEM((CHUNKS, BAL, WIDTH), bf16),
            pltpu.VMEM((CHUNKS, 2 * FAR, WIDTH), bf16),
            pltpu.VMEM((CHUNKS, BAL, WIDTH), bf16),
            pltpu.VMEM((CHUNKS, 2 * FAR, WIDTH), bf16),
            pltpu.VMEM((SLABS, 2 * HD), bf16),
            pltpu.VMEM((2 * HD, SLABS), bf16),
            pltpu.VMEM((BAL, SLABS), bf16),
            pltpu.VMEM((SLABS, BAL), bf16),
            pltpu.VMEM((STEPS, ROWS, STEP), f32),
            pltpu.VMEM((STEPS, CHUNKS * ROWS, STEP), bf16),
            pltpu.VMEM((STEPS, CHUNKS * ROWS, STEP), bf16),
            pltpu.VMEM((CHUNKS * ROWS, HD), bf16),
            pltpu.VMEM((CHUNKS * ROWS, HD), bf16),
            pltpu.VMEM((2 * HD, queries.shape[1]), bf16),
            pltpu.SemaphoreType.REGULAR,
            dma((4,)),
            dma((CHUNKS,)), dma((CHUNKS,)), dma, dma,
            dma((CHUNKS,)), dma((CHUNKS,)), dma((CHUNKS,)), dma((CHUNKS,)),
            dma((CHUNKS,)), dma((CHUNKS,)),
        ],
        compiler_params=pltpu.CompilerParams(
            collective_id=0, has_side_effects=True, vmem_limit_bytes=59 * 1024 * 1024
        ),
    )(
        block_image, image_owner, image_tiles, row_dest.reshape(1, -1), row_slot.reshape(1, -1),
        queries, grad_out, img_keys, img_values,
    )
    return pl.pallas_call(
        finish,
        out_shape=shapes,
        in_specs=[hbm] * 4,
        out_specs=(hbm,) * 4,
        scratch_shapes=[dma((4,))],
        compiler_params=pltpu.CompilerParams(vmem_limit_bytes=1024 * 1024),
    )(*results)


def solution(mesh):
    return jax.shard_map(
        shards,
        mesh=mesh,
        in_specs=(
            P("dp", "mp"),
            P("dp", "mp"),
            P("dp"),
            P("dp"),
            P("dp"),
            P(),
            P("dp"),
            P("dp", None, "mp"),
            P("dp", None, "mp"),
        ),
        out_specs=(P("dp", "mp"), P("dp", "mp"), P("dp", None, "mp"), P("dp", None, "mp")),
        check_vma=False,
    )
```

```python
import functools

import jax
import jax.numpy as jnp
from jax import lax
from jax.experimental import pallas as pl
from jax.experimental.pallas import tpu as pltpu
from jax.sharding import PartitionSpec as P

HD = 128
TILE_TOK = 1601
TOKP = 1664
KEYS = 6656
SCALE = HD**-0.5
LOG2E = 1.4426950408889634
RANKS = 32
CHUNKS = 4
WIDTH = 256
SLAB = 16
SLABS = RANKS * SLAB
OWN = 96
FAR = 64
BAL = 2 * (OWN + FAR)
ROWS = 2 * (OWN + FAR)
STEP = 3328
STEPS = KEYS // STEP
AHEAD = 2
MESH = pl.DeviceIdType.MESH
f32 = jnp.float32
bf16 = jnp.bfloat16
NT = ((1,), (1,))
NN = ((1,), (0,))


def dot(a, b, dims=NN):
    return lax.dot_general(a, b, (dims, ((), ())), preferred_element_type=f32)


def iota(shape, dim):
    return lax.broadcasted_iota(jnp.int32, shape, dim)


def fold(x, op):
    r = x[:, :HD]
    for i in range(1, x.shape[1] // HD):
        r = op(r, x[:, i * HD : (i + 1) * HD])
    return r


def as_column(row, n):
    return jnp.transpose(jnp.broadcast_to(row, (HD, n)))[:, :1]


def kernel(
    image_ref, owner_ref, tiles_ref, dest_ref, slot_ref, q_ref, g_ref, k_ref, v_ref,
    att_ref, gq_ref, k_buf, v_buf,
    snd, rcv, rep, ret, tab, tab_in, bal, far, res, back,
    pack, unpack, place, unplace, scores, weights, slopes, q_low, g_low, rows,
    entered, held, in_send, in_recv, tab_send, tab_recv, far_send, far_recv, back_send, back_recv, out_send, out_recv,
):
    me = lax.axis_index("dp")
    mz, mx = me >> 2, me & 3

    def ahead(k):
        return {"dp": ((mz + k // 4) & 7) * 4 + ((mx + k % 4) & 3)}

    def behind(k):
        return {"dp": ((mz + 8 - k // 4) & 7) * 4 + ((mx + 4 - k % 4) & 3)}

    nxt = {"dp": (me + 1) & (RANKS - 1)}
    prv = {"dp": (me + RANKS - 1) & (RANKS - 1)}
    barrier = pltpu.get_barrier_semaphore()
    get_k = pltpu.make_async_copy(k_ref, k_buf, held.at[0])
    get_v = pltpu.make_async_copy(v_ref, v_buf, held.at[1])
    get_q = pltpu.make_async_copy(q_ref, rows.at[pl.ds(0, HD)], held.at[2])
    get_g = pltpu.make_async_copy(g_ref, rows.at[pl.ds(HD, HD)], held.at[3])
    get_q.start()
    get_g.start()
    get_k.start()
    get_v.start()

    lines = [k for k in range(1, RANKS) if k < 4 or k % 4 == 0]
    for k in lines:
        pl.semaphore_signal(barrier, 1, device_id=ahead(k), device_id_type=MESH)

    dest = dest_ref[...]
    slot = slot_ref[...]
    offset = (((dest >> 2) - mz) & 7) * 4 + (((dest & 3) - mx) & 3)
    dest_c = as_column(dest, HD)
    same = (dest_c == dest) & (iota((HD, HD), 0) < iota((HD, HD), 1))
    position = jnp.sum(same.astype(jnp.int32), axis=0, keepdims=True)
    target = jnp.concatenate([offset * SLAB + position, offset * SLAB + 8 + position], axis=1)
    pack[...] = (iota((SLABS, 2 * HD), 0) == target).astype(bf16)
    position_c = as_column(position, HD)
    slot_c = as_column(slot, HD)
    which = (iota((RANKS, HD), 0) == offset).astype(bf16)
    named = jnp.where(position_c == (iota((HD, HD), 1) & 7), slot_c + 1, 0).astype(bf16)
    tab[...] = dot(which, named)

    def fill(c):
        cols = slice(c * WIDTH, (c + 1) * WIDTH)
        snd[c] = dot(pack[...], rows[:, cols]).astype(bf16)
        rcv[c, 0:SLAB] = snd[c, 0:SLAB]

    get_q.wait()
    get_g.wait()
    fill(0)
    tab_in[0:1] = tab[0:1]
    pl.semaphore_wait(barrier, len(lines))
    for k in range(1, 4):
        pl.semaphore_signal(entered, 1, device_id=ahead(k), device_id_type=MESH)
    pl.semaphore_wait(entered, 3)

    def slab(k):
        return pl.ds(k * SLAB, SLAB)

    def send_in(c):
        for k in range(1, RANKS):
            pltpu.make_async_remote_copy(
                snd.at[c, slab(k)], rcv.at[c, slab(k)], in_send.at[c], in_recv.at[c],
                device_id=ahead(k), device_id_type=MESH,
            ).start()

    send_in(0)
    for k in range(1, RANKS):
        pltpu.make_async_remote_copy(
            tab.at[pl.ds(k, 1)], tab_in.at[pl.ds(k, 1)], tab_send, tab_recv,
            device_id=ahead(k), device_id_type=MESH,
        ).start()
    for c in range(1, AHEAD):
        fill(c)
        send_in(c)
    for c in range(AHEAD, CHUNKS):
        fill(c)
    unpack[...] = (as_column(target, 2 * HD) == iota((2 * HD, SLABS), 1)).astype(bf16)

    rest = pl.ds(1, RANKS - 1)
    pltpu.make_async_copy(tab.at[rest], tab_in.at[rest], tab_recv).wait()
    pltpu.make_async_copy(tab.at[rest], tab_in.at[rest], tab_send).wait()
    spread = jnp.broadcast_to(tab_in[...][:, None, :], (RANKS, SLAB, HD))
    pick = iota((RANKS, SLAB, HD), 2) == (iota((RANKS, SLAB, HD), 1) & 7)
    got = jnp.sum(jnp.where(pick, spread, 0.0), axis=2, keepdims=True)
    got = got.reshape(SLABS, 1).astype(jnp.int32) - 1
    is_far = [(owner_ref[image_ref[b]] != me).astype(jnp.int32) for b in range(4)]
    seat = jnp.full((SLABS, 1), -1, jnp.int32)
    half = (iota((SLABS, 1), 0) >> 3) & 1
    owns, fars = 0, 0
    for b in range(4):
        own_row = owns * 32 + half * OWN
        far_row = 2 * OWN + fars * 32 + half * FAR
        base = own_row + (far_row - own_row) * is_far[b]
        seat = jnp.where((got >> 5) == b, base + (got & 31), seat)
        fars = fars + is_far[b]
        owns = owns + 1 - is_far[b]
    unplace[...] = (seat == iota((SLABS, BAL), 1)).astype(bf16)
    seat_r = jnp.transpose(jnp.broadcast_to(seat, (SLABS, HD)))[:1]
    place[...] = (iota((BAL, SLABS), 0) == seat_r).astype(bf16)

    all_but_first = pl.ds(SLAB, SLABS - SLAB)
    far_rows = pl.ds(2 * OWN, 2 * FAR)

    def far_copy(c):
        return pltpu.make_async_remote_copy(
            bal.at[c, far_rows], far.at[c], far_send.at[c], far_recv.at[c],
            device_id=nxt, device_id_type=MESH,
        )

    def back_copy(c):
        return pltpu.make_async_remote_copy(
            back.at[c], res.at[c, far_rows], back_send.at[c], back_recv.at[c],
            device_id=prv, device_id_type=MESH,
        )

    def take_in(c):
        pltpu.make_async_copy(snd.at[c, all_but_first], rcv.at[c, all_but_first], in_recv.at[c]).wait()
        bal[c, 2 * OWN :] = dot(place[2 * OWN :], rcv[c]).astype(bf16)
        far_copy(c).start()

        if isinstance(c, int):
            if c + AHEAD < CHUNKS:
                send_in(c + AHEAD)
        else:

            @pl.when(c + AHEAD < CHUNKS)
            def _():
                send_in(c + AHEAD)

        bal[c, : 2 * OWN] = dot(place[: 2 * OWN], rcv[c]).astype(bf16)

    def send_out(c):
        back_copy(c).wait_recv()
        rep[c] = dot(unplace[...], res[c]).astype(bf16)

        for k in range(1, RANKS):
            pltpu.make_async_remote_copy(
                rep.at[c, slab(k)], ret.at[c, slab(k)], out_send.at[c], out_recv.at[c],
                device_id=behind(k), device_id_type=MESH,
            ).start()

        ret[c, 0:SLAB] = rep[c, 0:SLAB]

    def segments(group):
        own = [(bal, res, 0, OWN, OWN, h) for h in range(2)]
        away = [(far, back, 0, FAR, FAR, h) for h in range(2)]
        return {"own": own, "far": away, "all": own + away}[group]

    def gather_rows(c, group, second):
        parts = []
        for src, _, first, other, n, h in segments(group):
            at = other if second else first
            parts.append(src[c, at : at + n, h * HD : (h + 1) * HD])
        return jnp.concatenate(parts, axis=0)

    def put_rows(c, group, second, x):
        top = 0
        for _, dst, first, other, n, h in segments(group):
            at = other if second else first
            dst[c, at : at + n, h * HD : (h + 1) * HD] = x[top : top + n]
            top += n

    def keys_of(j):
        return pl.ds(pl.multiple_of(j * STEP, STEP), STEP)

    count = tiles_ref[0]
    take_in(0)
    get_k.wait()
    get_v.wait()

    def attend(c, group, between=None):
        low_at = 2 * OWN if group == "far" else 0
        n = {"own": 2 * OWN, "far": 2 * FAR, "all": ROWS}[group]
        pairs = pl.ds(pl.multiple_of(c * ROWS + low_at, 64), n)
        q = gather_rows(c, group, False)
        g = gather_rows(c, group, True)

        def score_step(j, top):
            s = dot(q, k_buf[0, keys_of(j), :], NT)
            at = iota((1, STEP), 1) + j * STEP
            valid = (at % TOKP < TILE_TOK) & (at // TOKP < count)
            s = s + jnp.where(valid, 0.0, -1e30)
            scores[j, :n] = s
            return jnp.maximum(top, fold(s, jnp.maximum))

        top = lax.fori_loop(0, STEPS, score_step, jnp.full((n, HD), -3e38, f32))
        top = jnp.max(top, axis=1, keepdims=True) * (SCALE * LOG2E)
        if between is not None:
            between()

        def out_step(j, carry):
            total, out = carry
            e = jnp.exp2(scores[j, :n] * (SCALE * LOG2E) - top)
            low = e.astype(bf16)
            weights[j, pairs] = low
            return total + fold(e, jnp.add), out + dot(low, v_buf[0, keys_of(j), :])

        zeros = jnp.zeros((n, HD), f32)
        total, out = lax.fori_loop(0, STEPS, out_step, (zeros, zeros))
        inverse = 1.0 / jnp.sum(total, axis=1, keepdims=True)
        out = out * inverse
        put_rows(c, group, False, out.astype(bf16))
        g32 = g.astype(f32)
        delta = jnp.sum(g32 * out, axis=1, keepdims=True)
        g_low[pairs] = (g32 * inverse).astype(bf16)
        q_low[pairs] = (q.astype(f32) * (inverse * SCALE)).astype(bf16)

        def grad_step(j, grad_q):
            dp = dot(g, v_buf[0, keys_of(j), :], NT)
            ds = (weights[j, pairs].astype(f32) * (dp - delta)).astype(bf16)
            slopes[j, pairs] = ds
            return grad_q + dot(ds, k_buf[0, keys_of(j), :])

        grad_q = lax.fori_loop(0, STEPS, grad_step, zeros)
        put_rows(c, group, True, (grad_q * (inverse * SCALE)).astype(bf16))

    attend(0, "own")
    far_copy(0).wait_recv()
    attend(0, "far", lambda: take_in(1))
    back_copy(0).start()

    @pl.loop(1, CHUNKS - 1)
    def _(c):
        far_copy(c).wait_recv()
        attend(c, "all", lambda: take_in(c + 1))
        back_copy(c).start()
        send_out(c - 1)

    last = CHUNKS - 1
    far_copy(last).wait_recv()
    attend(last, "far")
    back_copy(last).start()
    send_out(last - 1)
    attend(last, "own")
    send_out(last)

    g_t = jnp.transpose(g_low[...].astype(f32)).astype(bf16)
    q_t = jnp.transpose(q_low[...].astype(f32)).astype(bf16)
    for j in range(STEPS):
        mine = slice(j * STEP, (j + 1) * STEP)
        k_buf[0, mine] = jnp.transpose(dot(q_t, slopes[j])).astype(bf16)
        v_buf[0, mine] = jnp.transpose(dot(g_t, weights[j])).astype(bf16)

    for c in range(CHUNKS):
        pltpu.make_async_copy(rep.at[c, all_but_first], ret.at[c, all_but_first], out_recv.at[c]).wait()
        final = dot(unpack[...], ret[c]).astype(bf16)
        cols = slice(c * WIDTH, (c + 1) * WIDTH)
        att_ref[:, cols] = final[:HD]
        gq_ref[:, cols] = final[HD:]

    for c in range(CHUNKS):
        pltpu.make_async_copy(snd.at[c, all_but_first], rcv.at[c, all_but_first], in_send.at[c]).wait()
        pltpu.make_async_copy(rep.at[c, all_but_first], ret.at[c, all_but_first], out_send.at[c]).wait()
        far_copy(c).wait_send()
        back_copy(c).wait_send()


def finish(*refs):
    copies = [
        pltpu.make_async_copy(src, dst, refs[-1].at[i])
        for i, (src, dst) in enumerate(zip(refs[:4], refs[4:8]))
    ]
    for copy in copies:
        copy.start()
    for copy in copies:
        copy.wait()


def shards(queries, grad_out, row_dest, row_slot, block_image, image_owner, image_tiles, img_keys, img_values):
    vmem = pl.BlockSpec(memory_space=pltpu.VMEM)
    smem = pl.BlockSpec(memory_space=pltpu.SMEM)
    hbm = pl.BlockSpec(memory_space=pl.ANY)
    dma = pltpu.SemaphoreType.DMA
    slabs = pltpu.VMEM((CHUNKS, SLABS, WIDTH), bf16)
    shapes = tuple(jax.ShapeDtypeStruct(x.shape, bf16) for x in (queries, grad_out, img_keys, img_values))
    results = pl.pallas_call(
        kernel,
        out_shape=tuple(pltpu.VMEM(x.shape, bf16) for x in shapes),
        in_specs=[smem] * 3 + [vmem] * 2 + [hbm] * 4,
        out_specs=(vmem,) * 4,
        scratch_shapes=[
            slabs, slabs, slabs, slabs,
            pltpu.VMEM((RANKS, HD), f32),
            pltpu.VMEM((RANKS, HD), f32),
            pltpu.VMEM((CHUNKS, BAL, WIDTH), bf16),
            pltpu.VMEM((CHUNKS, 2 * FAR, WIDTH), bf16),
            pltpu.VMEM((CHUNKS, BAL, WIDTH), bf16),
            pltpu.VMEM((CHUNKS, 2 * FAR, WIDTH), bf16),
            pltpu.VMEM((SLABS, 2 * HD), bf16),
            pltpu.VMEM((2 * HD, SLABS), bf16),
            pltpu.VMEM((BAL, SLABS), bf16),
            pltpu.VMEM((SLABS, BAL), bf16),
            pltpu.VMEM((STEPS, ROWS, STEP), f32),
            pltpu.VMEM((STEPS, CHUNKS * ROWS, STEP), bf16),
            pltpu.VMEM((STEPS, CHUNKS * ROWS, STEP), bf16),
            pltpu.VMEM((CHUNKS * ROWS, HD), bf16),
            pltpu.VMEM((CHUNKS * ROWS, HD), bf16),
            pltpu.VMEM((2 * HD, queries.shape[1]), bf16),
            pltpu.SemaphoreType.REGULAR,
            dma((4,)),
            dma((CHUNKS,)), dma((CHUNKS,)), dma, dma,
            dma((CHUNKS,)), dma((CHUNKS,)), dma((CHUNKS,)), dma((CHUNKS,)),
            dma((CHUNKS,)), dma((CHUNKS,)),
        ],
        compiler_params=pltpu.CompilerParams(
            collective_id=0, has_side_effects=True, vmem_limit_bytes=59 * 1024 * 1024
        ),
    )(
        block_image, image_owner, image_tiles, row_dest.reshape(1, -1), row_slot.reshape(1, -1),
        queries, grad_out, img_keys, img_values,
    )
    return pl.pallas_call(
        finish,
        out_shape=shapes,
        in_specs=[hbm] * 4,
        out_specs=(hbm,) * 4,
        scratch_shapes=[dma((4,))],
        compiler_params=pltpu.CompilerParams(vmem_limit_bytes=1024 * 1024),
    )(*results)


def solution(mesh):
    return jax.shard_map(
        shards,
        mesh=mesh,
        in_specs=(
            P("dp", "mp"),
            P("dp", "mp"),
            P("dp"),
            P("dp"),
            P("dp"),
            P(),
            P("dp"),
            P("dp", None, "mp"),
            P("dp", None, "mp"),
        ),
        out_specs=(P("dp", "mp"), P("dp", "mp"), P("dp", None, "mp"), P("dp", None, "mp")),
        check_vma=False,
    )
```

```python
import functools

import jax
import jax.numpy as jnp
from jax import lax
from jax.experimental import pallas as pl
from jax.experimental.pallas import tpu as pltpu
from jax.sharding import PartitionSpec as P

HD = 128
TILE_TOK = 1601
TOKP = 1664
KEYS = 6656
SCALE = HD**-0.5
LOG2E = 1.4426950408889634
RANKS = 32
CHUNKS = 4
WIDTH = 256
SLAB = 16
SLABS = RANKS * SLAB
OWN = 96
FAR = 64
BAL = 2 * (OWN + FAR)
ROWS = 2 * (OWN + FAR)
STEP = 3328
STEPS = KEYS // STEP
AHEAD = 2
MESH = pl.DeviceIdType.MESH
f32 = jnp.float32
bf16 = jnp.bfloat16
NT = ((1,), (1,))
NN = ((1,), (0,))


def dot(a, b, dims=NN):
    return lax.dot_general(a, b, (dims, ((), ())), preferred_element_type=f32)


def iota(shape, dim):
    return lax.broadcasted_iota(jnp.int32, shape, dim)


def fold(x, op):
    r = x[:, :HD]
    for i in range(1, x.shape[1] // HD):
        r = op(r, x[:, i * HD : (i + 1) * HD])
    return r


def as_column(row, n):
    return jnp.transpose(jnp.broadcast_to(row, (HD, n)))[:, :1]


def kernel(
    image_ref, owner_ref, tiles_ref, dest_ref, slot_ref, q_ref, g_ref, k_ref, v_ref,
    att_ref, gq_ref, k_buf, v_buf,
    snd, rcv, rep, ret, tab, tab_in, bal, far, res, back,
    pack, unpack, place, unplace, scores, weights, slopes, q_low, g_low, rows,
    entered, held, in_send, in_recv, tab_send, tab_recv, far_send, far_recv, back_send, back_recv, out_send, out_recv,
):
    me = lax.axis_index("dp")
    mz, mx = me >> 2, me & 3

    def ahead(k):
        return {"dp": ((mz + k // 4) & 7) * 4 + ((mx + k % 4) & 3)}

    def behind(k):
        return {"dp": ((mz + 8 - k // 4) & 7) * 4 + ((mx + 4 - k % 4) & 3)}

    nxt = {"dp": (me + 1) & (RANKS - 1)}
    prv = {"dp": (me + RANKS - 1) & (RANKS - 1)}
    barrier = pltpu.get_barrier_semaphore()
    get_k = pltpu.make_async_copy(k_ref, k_buf, held.at[0])
    get_v = pltpu.make_async_copy(v_ref, v_buf, held.at[1])
    get_q = pltpu.make_async_copy(q_ref, rows.at[pl.ds(0, HD)], held.at[2])
    get_g = pltpu.make_async_copy(g_ref, rows.at[pl.ds(HD, HD)], held.at[3])
    get_q.start()
    get_g.start()
    get_k.start()
    get_v.start()

    lines = [k for k in range(1, RANKS) if k < 4 or k % 4 == 0]
    for k in lines:
        pl.semaphore_signal(barrier, 1, device_id=ahead(k), device_id_type=MESH)

    dest = dest_ref[...]
    slot = slot_ref[...]
    offset = (((dest >> 2) - mz) & 7) * 4 + (((dest & 3) - mx) & 3)
    dest_c = as_column(dest, HD)
    same = (dest_c == dest) & (iota((HD, HD), 0) < iota((HD, HD), 1))
    position = jnp.sum(same.astype(jnp.int32), axis=0, keepdims=True)
    target = jnp.concatenate([offset * SLAB + position, offset * SLAB + 8 + position], axis=1)
    pack[...] = (iota((SLABS, 2 * HD), 0) == target).astype(bf16)
    position_c = as_column(position, HD)
    slot_c = as_column(slot, HD)
    which = (iota((RANKS, HD), 0) == offset).astype(bf16)
    named = jnp.where(position_c == (iota((HD, HD), 1) & 7), slot_c + 1, 0).astype(bf16)
    tab[...] = dot(which, named)

    def fill(c):
        cols = slice(c * WIDTH, (c + 1) * WIDTH)
        snd[c] = dot(pack[...], rows[:, cols]).astype(bf16)
        rcv[c, 0:SLAB] = snd[c, 0:SLAB]

    get_q.wait()
    get_g.wait()
    fill(0)
    tab_in[0:1] = tab[0:1]
    pl.semaphore_wait(barrier, len(lines))
    for k in range(1, 4):
        pl.semaphore_signal(entered, 1, device_id=ahead(k), device_id_type=MESH)
    pl.semaphore_wait(entered, 3)

    def slab(k):
        return pl.ds(k * SLAB, SLAB)

    def send_in(c):
        for k in range(1, RANKS):
            pltpu.make_async_remote_copy(
                snd.at[c, slab(k)], rcv.at[c, slab(k)], in_send.at[c], in_recv.at[c],
                device_id=ahead(k), device_id_type=MESH,
            ).start()

    send_in(0)
    for k in range(1, RANKS):
        pltpu.make_async_remote_copy(
            tab.at[pl.ds(k, 1)], tab_in.at[pl.ds(k, 1)], tab_send, tab_recv,
            device_id=ahead(k), device_id_type=MESH,
        ).start()
    for c in range(1, AHEAD):
        fill(c)
        send_in(c)
    for c in range(AHEAD, CHUNKS):
        fill(c)
    unpack[...] = (as_column(target, 2 * HD) == iota((2 * HD, SLABS), 1)).astype(bf16)

    rest = pl.ds(1, RANKS - 1)
    pltpu.make_async_copy(tab.at[rest], tab_in.at[rest], tab_recv).wait()
    pltpu.make_async_copy(tab.at[rest], tab_in.at[rest], tab_send).wait()
    spread = jnp.broadcast_to(tab_in[...][:, None, :], (RANKS, SLAB, HD))
    pick = iota((RANKS, SLAB, HD), 2) == (iota((RANKS, SLAB, HD), 1) & 7)
    got = jnp.sum(jnp.where(pick, spread, 0.0), axis=2, keepdims=True)
    got = got.reshape(SLABS, 1).astype(jnp.int32) - 1
    is_far = [(owner_ref[image_ref[b]] != me).astype(jnp.int32) for b in range(4)]
    seat = jnp.full((SLABS, 1), -1, jnp.int32)
    half = (iota((SLABS, 1), 0) >> 3) & 1
    owns, fars = 0, 0
    for b in range(4):
        own_row = owns * 32 + half * OWN
        far_row = 2 * OWN + fars * 32 + half * FAR
        base = own_row + (far_row - own_row) * is_far[b]
        seat = jnp.where((got >> 5) == b, base + (got & 31), seat)
        fars = fars + is_far[b]
        owns = owns + 1 - is_far[b]
    unplace[...] = (seat == iota((SLABS, BAL), 1)).astype(bf16)
    seat_r = jnp.transpose(jnp.broadcast_to(seat, (SLABS, HD)))[:1]
    place[...] = (iota((BAL, SLABS), 0) == seat_r).astype(bf16)

    all_but_first = pl.ds(SLAB, SLABS - SLAB)
    far_rows = pl.ds(2 * OWN, 2 * FAR)

    def far_copy(c):
        return pltpu.make_async_remote_copy(
            bal.at[c, far_rows], far.at[c], far_send.at[c], far_recv.at[c],
            device_id=nxt, device_id_type=MESH,
        )

    def back_copy(c):
        return pltpu.make_async_remote_copy(
            back.at[c], res.at[c, far_rows], back_send.at[c], back_recv.at[c],
            device_id=prv, device_id_type=MESH,
        )

    def take_in(c):
        pltpu.make_async_copy(snd.at[c, all_but_first], rcv.at[c, all_but_first], in_recv.at[c]).wait()
        bal[c, 2 * OWN :] = dot(place[2 * OWN :], rcv[c]).astype(bf16)
        far_copy(c).start()

        if isinstance(c, int):
            if c + AHEAD < CHUNKS:
                send_in(c + AHEAD)
        else:

            @pl.when(c + AHEAD < CHUNKS)
            def _():
                send_in(c + AHEAD)

        bal[c, : 2 * OWN] = dot(place[: 2 * OWN], rcv[c]).astype(bf16)

    def send_out(c):
        back_copy(c).wait_recv()
        rep[c] = dot(unplace[...], res[c]).astype(bf16)

        for k in sorted(range(1, RANKS), key=lambda k: -min(k // 4, 8 - k // 4) - min(k % 4, 4 - k % 4)):
            pltpu.make_async_remote_copy(
                rep.at[c, slab(k)], ret.at[c, slab(k)], out_send.at[c], out_recv.at[c],
                device_id=behind(k), device_id_type=MESH,
            ).start()

        ret[c, 0:SLAB] = rep[c, 0:SLAB]

    def segments(group):
        own = [(bal, res, 0, OWN, OWN, h) for h in range(2)]
        away = [(far, back, 0, FAR, FAR, h) for h in range(2)]
        return {"own": own, "far": away, "all": own + away}[group]

    def gather_rows(c, group, second):
        parts = []
        for src, _, first, other, n, h in segments(group):
            at = other if second else first
            parts.append(src[c, at : at + n, h * HD : (h + 1) * HD])
        return jnp.concatenate(parts, axis=0)

    def put_rows(c, group, second, x):
        top = 0
        for _, dst, first, other, n, h in segments(group):
            at = other if second else first
            dst[c, at : at + n, h * HD : (h + 1) * HD] = x[top : top + n]
            top += n

    def keys_of(j):
        return pl.ds(pl.multiple_of(j * STEP, STEP), STEP)

    count = tiles_ref[0]
    take_in(0)
    get_k.wait()
    get_v.wait()

    def attend(c, group, between=None):
        low_at = 2 * OWN if group == "far" else 0
        n = {"own": 2 * OWN, "far": 2 * FAR, "all": ROWS}[group]
        pairs = pl.ds(pl.multiple_of(c * ROWS + low_at, 64), n)
        q = gather_rows(c, group, False)
        g = gather_rows(c, group, True)

        def score_step(j, top):
            s = dot(q, k_buf[0, keys_of(j), :], NT)
            at = iota((1, STEP), 1)
            second = (at >= TOKP).astype(jnp.int32)
            valid = (at - second * TOKP < TILE_TOK) & (j * (STEP // TOKP) + second < count)
            s = s + jnp.where(valid, 0.0, -1e30)
            scores[j, :n] = s
            return jnp.maximum(top, fold(s, jnp.maximum))

        top = lax.fori_loop(0, STEPS, score_step, jnp.full((n, HD), -3e38, f32))
        top = jnp.max(top, axis=1, keepdims=True) * (SCALE * LOG2E)
        if between is not None:
            between()

        def out_step(j, carry):
            total, out = carry
            e = jnp.exp2(scores[j, :n] * (SCALE * LOG2E) - top)
            low = e.astype(bf16)
            weights[j, pairs] = low
            return total + fold(e, jnp.add), out + dot(low, v_buf[0, keys_of(j), :])

        zeros = jnp.zeros((n, HD), f32)
        total, out = lax.fori_loop(0, STEPS, out_step, (zeros, zeros))
        inverse = 1.0 / jnp.sum(total, axis=1, keepdims=True)
        out = out * inverse
        put_rows(c, group, False, out.astype(bf16))
        g32 = g.astype(f32)
        delta = jnp.sum(g32 * out, axis=1, keepdims=True)
        g_low[pairs] = (g32 * inverse).astype(bf16)
        q_low[pairs] = (q.astype(f32) * (inverse * SCALE)).astype(bf16)

        def grad_step(j, grad_q):
            dp = dot(g, v_buf[0, keys_of(j), :], NT)
            ds = (weights[j, pairs].astype(f32) * (dp - delta)).astype(bf16)
            slopes[j, pairs] = ds
            return grad_q + dot(ds, k_buf[0, keys_of(j), :])

        grad_q = lax.fori_loop(0, STEPS, grad_step, zeros)
        put_rows(c, group, True, (grad_q * (inverse * SCALE)).astype(bf16))

    attend(0, "own")
    far_copy(0).wait_recv()
    attend(0, "far", lambda: take_in(1))
    back_copy(0).start()

    @pl.loop(1, CHUNKS - 1)
    def _(c):
        far_copy(c).wait_recv()
        attend(c, "all", lambda: take_in(c + 1))
        back_copy(c).start()
        send_out(c - 1)

    last = CHUNKS - 1
    far_copy(last).wait_recv()
    attend(last, "far")
    back_copy(last).start()
    send_out(last - 1)
    attend(last, "own")
    send_out(last)

    g_t = jnp.transpose(g_low[...].astype(f32)).astype(bf16)
    q_t = jnp.transpose(q_low[...].astype(f32)).astype(bf16)
    for j in range(STEPS):
        mine = slice(j * STEP, (j + 1) * STEP)
        k_buf[0, mine] = jnp.transpose(dot(q_t, slopes[j])).astype(bf16)
        v_buf[0, mine] = jnp.transpose(dot(g_t, weights[j])).astype(bf16)

    for c in range(CHUNKS):
        pltpu.make_async_copy(rep.at[c, all_but_first], ret.at[c, all_but_first], out_recv.at[c]).wait()
        final = dot(unpack[...], ret[c]).astype(bf16)
        cols = slice(c * WIDTH, (c + 1) * WIDTH)
        att_ref[:, cols] = final[:HD]
        gq_ref[:, cols] = final[HD:]

    for c in range(CHUNKS):
        pltpu.make_async_copy(snd.at[c, all_but_first], rcv.at[c, all_but_first], in_send.at[c]).wait()
        pltpu.make_async_copy(rep.at[c, all_but_first], ret.at[c, all_but_first], out_send.at[c]).wait()
        far_copy(c).wait_send()
        back_copy(c).wait_send()


def finish(*refs):
    copies = [
        pltpu.make_async_copy(src, dst, refs[-1].at[i])
        for i, (src, dst) in enumerate(zip(refs[:4], refs[4:8]))
    ]
    for copy in copies:
        copy.start()
    for copy in copies:
        copy.wait()


def shards(queries, grad_out, row_dest, row_slot, block_image, image_owner, image_tiles, img_keys, img_values):
    vmem = pl.BlockSpec(memory_space=pltpu.VMEM)
    smem = pl.BlockSpec(memory_space=pltpu.SMEM)
    hbm = pl.BlockSpec(memory_space=pl.ANY)
    dma = pltpu.SemaphoreType.DMA
    slabs = pltpu.VMEM((CHUNKS, SLABS, WIDTH), bf16)
    shapes = tuple(jax.ShapeDtypeStruct(x.shape, bf16) for x in (queries, grad_out, img_keys, img_values))
    results = pl.pallas_call(
        kernel,
        out_shape=tuple(pltpu.VMEM(x.shape, bf16) for x in shapes),
        in_specs=[smem] * 3 + [vmem] * 2 + [hbm] * 4,
        out_specs=(vmem,) * 4,
        scratch_shapes=[
            slabs, slabs, slabs, slabs,
            pltpu.VMEM((RANKS, HD), f32),
            pltpu.VMEM((RANKS, HD), f32),
            pltpu.VMEM((CHUNKS, BAL, WIDTH), bf16),
            pltpu.VMEM((CHUNKS, 2 * FAR, WIDTH), bf16),
            pltpu.VMEM((CHUNKS, BAL, WIDTH), bf16),
            pltpu.VMEM((CHUNKS, 2 * FAR, WIDTH), bf16),
            pltpu.VMEM((SLABS, 2 * HD), bf16),
            pltpu.VMEM((2 * HD, SLABS), bf16),
            pltpu.VMEM((BAL, SLABS), bf16),
            pltpu.VMEM((SLABS, BAL), bf16),
            pltpu.VMEM((STEPS, ROWS, STEP), f32),
            pltpu.VMEM((STEPS, CHUNKS * ROWS, STEP), bf16),
            pltpu.VMEM((STEPS, CHUNKS * ROWS, STEP), bf16),
            pltpu.VMEM((CHUNKS * ROWS, HD), bf16),
            pltpu.VMEM((CHUNKS * ROWS, HD), bf16),
            pltpu.VMEM((2 * HD, queries.shape[1]), bf16),
            pltpu.SemaphoreType.REGULAR,
            dma((4,)),
            dma((CHUNKS,)), dma((CHUNKS,)), dma, dma,
            dma((CHUNKS,)), dma((CHUNKS,)), dma((CHUNKS,)), dma((CHUNKS,)),
            dma((CHUNKS,)), dma((CHUNKS,)),
        ],
        compiler_params=pltpu.CompilerParams(
            collective_id=0, has_side_effects=True, vmem_limit_bytes=59 * 1024 * 1024
        ),
    )(
        block_image, image_owner, image_tiles, row_dest.reshape(1, -1), row_slot.reshape(1, -1),
        queries, grad_out, img_keys, img_values,
    )
    return pl.pallas_call(
        finish,
        out_shape=shapes,
        in_specs=[hbm] * 4,
        out_specs=(hbm,) * 4,
        scratch_shapes=[dma((4,))],
        compiler_params=pltpu.CompilerParams(vmem_limit_bytes=1024 * 1024),
    )(*results)


def solution(mesh):
    return jax.shard_map(
        shards,
        mesh=mesh,
        in_specs=(
            P("dp", "mp"),
            P("dp", "mp"),
            P("dp"),
            P("dp"),
            P("dp"),
            P(),
            P("dp"),
            P("dp", None, "mp"),
            P("dp", None, "mp"),
        ),
        out_specs=(P("dp", "mp"), P("dp", "mp"), P("dp", None, "mp"), P("dp", None, "mp")),
        check_vma=False,
    )
```
